256 devices in a mesh: seq: 32 (over y, z), head: 8 (over x, core).
Axes of the slice: x: 4, y: 4, z: 8, core: 2. Of those that a mesh axis runs over, the one named last changes fastest.
Arguments:
- queries: bfloat16 [131072, 8, 256], P('seq', 'head'), may hold values from -6 to 6
- key_vectors: bfloat16 [131072, 8, 256], P('seq', 'head'), may hold values from -6 to 6
- value_vectors: bfloat16 [131072, 8, 512], P('seq', 'head'), may hold values from -21 to 21
- input_gate: float32 [8, 131072], P('head', 'seq'), may hold values from -90 to 150, as said below
- forget_gate: float32 [8, 131072], P('head', 'seq'), may hold values from -0.01 to 20, as said below
- norm_gain: float32 [4096], replicated, may hold values from 0.1 to 1.9
Outputs:
- cell_output: bfloat16 [131072, 4096], P(('seq', 'head'))
The draws below stay inside these ranges and needn't reach their ends.
Inputs may be any that keep to these rules, and one draw needn't show every extreme that they name: `input_gate`: input gate preactivations of every head and token. `forget_gate`: forget gate preactivations of every head and token.
All inputs are finite; a program needn't handle non-finite values.
Results may differ from the reference program's by a relative error of at most 0.02.
Values may be sent and summed in bfloat16 or wider, within the bound.
No kernel may reach another device: no remote copies, remote signals or barrier semaphores. Data moves between devices by JAX's collectives and lax.ppermute only.
A program may use at most 128 MiB of HBM per device.

```python
import math
import jax
import jax.numpy as jnp
from jax import lax

HEAD_COUNT = 8
DK = 256
DV = 512
CH = 64
TOK_DEV = 4096
DOCUMENT_TOKENS = 131072


def draw_value_vectors(key, part):
    key = jax.random.fold_in(key, 11)
    col_key, base_key = jax.random.split(key, 2)
    column_scale = jnp.exp(jax.random.uniform(col_key, (1, HEAD_COUNT, DV), jnp.float32, math.log(0.3), math.log(3.0)))
    base_draw = jnp.clip(jax.random.normal(base_key, (DOCUMENT_TOKENS, HEAD_COUNT, DV), jnp.float32), -6.0, 6.0)
    values = base_draw * column_scale
    return values.astype(jnp.bfloat16)


def draw_input_gate(key, part):
    key = jax.random.fold_in(key, 23)
    base_key = jax.random.fold_in(key, 0)
    gate_draw = jnp.clip(1.5 * jax.random.normal(base_key, (HEAD_COUNT, DOCUMENT_TOKENS), jnp.float32), -9.0, 9.0)
    return gate_draw


def draw_forget_gate(key, part):
    key = jax.random.fold_in(key, 37)
    permute_random_key, block_random_key, token_random_key, gradual_random_key, quick_random_key, surge_random_key, retain_random_key = jax.random.split(key, 7)
    order = jax.random.permutation(permute_random_key, HEAD_COUNT)
    fast_count = HEAD_COUNT // 2
    fast_head = (order < fast_count)[:, None]
    block_factor = jnp.exp(jax.random.uniform(block_random_key, (HEAD_COUNT, DOCUMENT_TOKENS // TOK_DEV), jnp.float32, math.log(0.5), math.log(2.0)))
    block_factor = jnp.repeat(block_factor, TOK_DEV, axis=1)
    token_factor = jax.random.uniform(token_random_key, (HEAD_COUNT, DOCUMENT_TOKENS), jnp.float32, 0.5, 1.5)
    slow_rate = jax.random.uniform(gradual_random_key, (HEAD_COUNT, 1), jnp.float32, 0.1, 0.5) / DOCUMENT_TOKENS
    fast_rate = 1.0 / jax.random.uniform(quick_random_key, (HEAD_COUNT, 1), jnp.float32, 30.0, 50.0)
    decay_speed = jnp.where(fast_head, fast_rate, slow_rate) * token_factor * block_factor
    surge_mask = jax.random.uniform(surge_random_key, (HEAD_COUNT, DOCUMENT_TOKENS), jnp.float32) < 2.0 / DOCUMENT_TOKENS
    retain_fraction = jax.random.uniform(retain_random_key, (HEAD_COUNT, DOCUMENT_TOKENS), jnp.float32, 0.5, 0.8)
    log_decay_factor = jnp.where(surge_mask, jnp.log(retain_fraction), -decay_speed)
    return -jnp.log(jnp.expm1(-log_decay_factor))


def block_scale(rng, shape, pieces, low, high):
    level = 1.0
    for dim, blocks in pieces:
        heights = jax.random.uniform(jax.random.fold_in(jax.random.fold_in(rng, 6), dim), (blocks,), jnp.float32, low / len(pieces), high / len(pieces))
        level = level * jnp.repeat(jnp.exp(heights), shape[dim] // blocks).reshape((-1,) + (1,) * (len(shape) - 1 - dim))
    return level


def gaussian(key, dims, scale, limit, shards=(), held_as=jnp.bfloat16):
    entries = scale * jax.random.normal(key, dims, jnp.float32)
    if shards:
        entries = entries * block_scale(key, dims, shards, -0.22, 0.18)
    return jnp.clip(entries, -limit, limit).astype(held_as)


def setup_inputs(seed: int = 0) -> dict:
    keys = jax.random.split(jax.random.key(seed), 7)
    queries = gaussian(keys[0], (DOCUMENT_TOKENS, HEAD_COUNT, DK), 1.0, 6.0, ((0, 32), (1, 8)))
    key_vectors = gaussian(keys[1], (DOCUMENT_TOKENS, HEAD_COUNT, DK), 1.0, 6.0, ((0, 32), (1, 8)))
    value_vectors = draw_value_vectors(jax.random.fold_in(keys[6], 71), 0)
    input_gate = draw_input_gate(jax.random.fold_in(keys[6], 71), 0)
    forget_gate = draw_forget_gate(jax.random.fold_in(keys[6], 71), 0)
    norm_gain = jnp.clip(1.0 + 0.18 * jax.random.normal(keys[5], (HEAD_COUNT * DV,), jnp.float32), 0.1, 1.9)
    return {"queries": queries, "key_vectors": key_vectors, "value_vectors": value_vectors, "input_gate": input_gate, "forget_gate": forget_gate, "norm_gain": norm_gain}


FLOOR_LOG = -1e+30

def split_pair(state):
    high = lax.optimization_barrier(state.astype(jnp.bfloat16))
    low = (state - high.astype(jnp.float32)).astype(jnp.bfloat16)
    return (high, low)

def fold_state(carried, block_parts):
    carry_matrix, carry_vector, carry_level = carried
    block_matrix, block_vector, block_top, block_total = block_parts
    shifted = carry_level + block_total
    new_level = jnp.maximum(shifted, block_top)
    old_scale = jnp.exp(shifted - new_level)
    new_scale = jnp.exp(block_top - new_level)
    return (old_scale * carry_matrix + new_scale * block_matrix, old_scale * carry_vector + new_scale * block_vector, new_level)

def one_head(query_all, key_all, value_all, input_all, forget_all):
    block_count = DOCUMENT_TOKENS // CH
    qk_scale = 1.0 / math.sqrt(DK)
    query_blocks = query_all.reshape(block_count, CH, DK)
    key_blocks = key_all.reshape(block_count, CH, DK)
    value_blocks = value_all.reshape(block_count, CH, DV)
    input_blocks = input_all.reshape(block_count, CH)
    decay_blocks = jax.nn.log_sigmoid(forget_all).reshape(block_count, CH)
    causal = jnp.arange(CH)[:, None] >= jnp.arange(CH)[None, :]

    def advance(carried, inputs):
        query_rows, key_rows, value_rows, input_rows, decay_rows = inputs
        within = jnp.cumsum(decay_rows)
        block_total = within[-1]
        key_log = block_total - within + input_rows
        key_top = jnp.max(key_log)
        weighted = (key_rows * jnp.exp(key_log - key_top)[:, None]).astype(jnp.bfloat16)
        block_matrix = jnp.dot(weighted.T, value_rows, preferred_element_type=jnp.float32)
        block_vector = lax.optimization_barrier(jnp.sum(weighted.astype(jnp.float32), axis=0))
        scores = jnp.dot(query_rows, key_rows.T, preferred_element_type=jnp.float32) * qk_scale
        pair_log = jnp.where(causal, within[:, None] - within[None, :] + input_rows[None, :], -jnp.inf)
        pair_top = lax.optimization_barrier(jnp.max(pair_log, axis=1))
        pair_probs = jnp.exp(pair_log - pair_top[:, None]) * scores
        intra_numer = jnp.dot(pair_probs.astype(jnp.bfloat16), value_rows, preferred_element_type=jnp.float32)
        intra_denom = lax.optimization_barrier(jnp.sum(pair_probs, axis=1))
        carry_matrix, carry_vector, carry_level = carried
        carry_log = within + carry_level
        row_level = jnp.maximum(pair_top, carry_log)
        matrix_high, matrix_low = split_pair(carry_matrix)
        vector_high, vector_low = split_pair(carry_vector)
        carry_numer = (jnp.dot(query_rows, matrix_high, preferred_element_type=jnp.float32) + jnp.dot(query_rows, matrix_low, preferred_element_type=jnp.float32)) * qk_scale
        carry_denom = (jnp.dot(query_rows, vector_high, preferred_element_type=jnp.float32) + jnp.dot(query_rows, vector_low, preferred_element_type=jnp.float32)) * qk_scale
        own_scale = jnp.exp(pair_top - row_level)
        far_scale = jnp.exp(carry_log - row_level)
        numerator = own_scale[:, None] * intra_numer + far_scale[:, None] * carry_numer
        denominator = own_scale * intra_denom + far_scale * carry_denom
        hidden_rows = (numerator / jnp.maximum(jnp.abs(denominator), 1.0)[:, None]).astype(jnp.bfloat16)
        updated = fold_state(carried, (block_matrix, block_vector, key_top, block_total))
        return (updated, hidden_rows)
    initial = (jnp.zeros((DK, DV), jnp.float32), jnp.zeros((DK,), jnp.float32), jnp.array(FLOOR_LOG, jnp.float32))
    finished, hidden_blocks = lax.scan(advance, initial, (query_blocks, key_blocks, value_blocks, input_blocks, decay_blocks))
    return hidden_blocks.reshape(DOCUMENT_TOKENS, DV)

def reference(queries, key_vectors, value_vectors, input_gate, forget_gate, norm_gain):

    def per_head(head_number):
        return one_head(lax.dynamic_index_in_dim(queries, head_number, 1, keepdims=False), lax.dynamic_index_in_dim(key_vectors, head_number, 1, keepdims=False), lax.dynamic_index_in_dim(value_vectors, head_number, 1, keepdims=False), lax.dynamic_index_in_dim(input_gate, head_number, 0, keepdims=False), lax.dynamic_index_in_dim(forget_gate, head_number, 0, keepdims=False))
    hidden = lax.map(per_head, jnp.arange(HEAD_COUNT, dtype=jnp.int32))
    hidden = jnp.transpose(hidden, (1, 0, 2)).reshape(DOCUMENT_TOKENS, HEAD_COUNT * DV)
    wide = hidden.astype(jnp.float32)
    factor = 1.0 / jnp.sqrt(lax.optimization_barrier(jnp.mean(wide * wide, axis=-1, keepdims=True)) + 1e-06)
    return (wide * factor * norm_gain).astype(jnp.bfloat16)
```

```python
import functools

import jax
import jax.numpy as jnp
from jax import lax
from jax.experimental import pallas as pl
from jax.experimental.pallas import tpu as pltpu
from jax.sharding import PartitionSpec as P

EPSILON = 1e-06
FLOOR_LOG = -1e30
L = 256
EXT = 128
BF = jnp.bfloat16
F32 = jnp.float32
VMEM_LIMIT = 48 * 1024 * 1024


def dot(a, b):
    return jnp.dot(a, b, preferred_element_type=F32)


def pieces(x):
    hi = x.astype(BF).astype(F32)
    rest = x - hi
    mid = rest.astype(BF).astype(F32)
    return hi, mid, rest - mid


def ones_column(rows):
    return jnp.where(lax.broadcasted_iota(jnp.int32, (rows, EXT), 1) == 0, 1.0, 0.0).astype(BF)


def lay_columns(rows, columns):
    lane = lax.broadcasted_iota(jnp.int32, (rows, EXT), 1)
    out = jnp.zeros((rows, EXT), F32)
    for number, column in enumerate(columns):
        out = jnp.where(lane == number, column, out)
    return out


def gate_rows(forget_ref, input_ref, gates_ref, weight_ref, ends_ref):
    chunks = forget_ref.shape[0] * 128 // L

    def rows(ref):
        return jnp.concatenate(
            [ref[pl.ds(0, chunks, stride=2), :], ref[pl.ds(1, chunks, stride=2), :]], axis=1
        )

    forget = rows(forget_ref)
    lgate = jnp.minimum(forget, 0.0) - jnp.log1p(jnp.exp(-jnp.abs(forget)))
    lane = lax.broadcasted_iota(jnp.int32, (chunks, L), 1)
    within = lgate
    shift = 1
    while shift < L:
        within = within + jnp.where(lane >= shift, pltpu.roll(within, shift, 1), 0.0)
        shift *= 2
    lead = rows(input_ref) - within
    top = lead
    shift = 1
    while shift < L:
        top = jnp.maximum(top, jnp.where(lane >= shift, pltpu.roll(top, shift, 1), -jnp.inf))
        shift *= 2
    total = within[:, L - 1 :]
    chunk_top = total + top[:, L - 1 :]
    row = lax.broadcasted_iota(jnp.int32, (chunks, 1), 0)
    level = jnp.full((1, 1), FLOOR_LOG, F32)
    before = jnp.zeros((1, 1), F32)
    enter = jnp.zeros((chunks, 1), F32)
    leave = jnp.zeros((chunks, 1), F32)
    prefix = jnp.zeros((chunks, 1), F32)
    for c in range(chunks):
        enter = jnp.where(row == c, level, enter)
        prefix = jnp.where(row == c, before, prefix)
        level = jnp.maximum(level + total[c : c + 1], chunk_top[c : c + 1])
        before = before + total[c : c + 1]
        leave = jnp.where(row == c, level, leave)
    after = jnp.zeros((1, 1), F32)
    suffix = jnp.zeros((chunks, 1), F32)
    for c in reversed(range(chunks)):
        suffix = jnp.where(row == c, after, suffix)
        after = after + total[c : c + 1]
    carry = within + enter
    levels = jnp.maximum(within + top, carry)
    keylog = lead + total
    weight_ref[...] = jnp.exp(keylog + suffix - level)
    ends_ref[0:1, :] = jnp.broadcast_to(level, (1, 128))
    ends_ref[1:2, :] = jnp.broadcast_to(before, (1, 128))

    def put(number, value):
        for half in range(2):
            gates_ref[pl.ds(half * 8 + number, chunks, stride=16), :] = value[:, half * 128 : (half + 1) * 128]

    put(0, within - levels)
    put(1, jnp.exp(carry - levels))
    put(2, lead)
    put(3, jnp.exp(keylog - leave))
    put(4, within + prefix)
    put(5, levels)
    put(6, jnp.broadcast_to(jnp.exp(enter + total - leave), (chunks, L)))
    put(7, jnp.zeros((chunks, L), F32))


def local_state(forget_ref, input_ref, key_ref, value_ref, packet_ref, gates_ref, weight_ref, ends_ref, total_ref):
    step = pl.program_id(0)
    width = value_ref.shape[1]
    per = key_ref.shape[0] // L

    @pl.when(step == 0)
    def _():
        gate_rows(forget_ref, input_ref, gates_ref, weight_ref, ends_ref)
        total_ref[...] = jnp.zeros_like(total_ref)

    ones = ones_column(L)
    for part in range(per):
        span = slice(part * L, (part + 1) * L)
        weight = weight_ref[pl.ds(step * per + part, 1), :]
        weighted = (key_ref[span, :].T.astype(F32) * weight).astype(BF)
        total_ref[:, :width] += dot(weighted, value_ref[span, :])
        total_ref[:, width:] += dot(weighted, ones)

    @pl.when(step == pl.num_programs(0) - 1)
    def _():
        rows = total_ref.shape[0]
        packet_ref[:, :width] = total_ref[:, :width].astype(BF)
        vector = pieces(total_ref[:, width : width + 1])
        level = pieces(ends_ref[0:1, 0:1])
        decay = pieces(ends_ref[1:2, 0:1])
        packet_ref[:, width:] = lay_columns(rows, vector[:2] + level + decay).astype(BF)


def run_local_state(forget, inputs, keys, values):
    tokens, depth = keys.shape
    width = values.shape[1]
    block = 512
    chunks = tokens // L
    return pl.pallas_call(
        local_state,
        grid=(tokens // block,),
        in_specs=[
            pl.BlockSpec((tokens // 128, 128), lambda i: (0, 0)),
            pl.BlockSpec((tokens // 128, 128), lambda i: (0, 0)),
            pl.BlockSpec((block, depth), lambda i: (i, 0)),
            pl.BlockSpec((block, width), lambda i: (i, 0)),
        ],
        out_specs=[
            pl.BlockSpec((depth, width + EXT), lambda i: (0, 0)),
            pl.BlockSpec((chunks * 16, 128), lambda i: (0, 0)),
        ],
        out_shape=[
            jax.ShapeDtypeStruct((depth, width + EXT), BF),
            jax.ShapeDtypeStruct((chunks * 16, 128), F32),
        ],
        scratch_shapes=[
            pltpu.VMEM((chunks, L), F32),
            pltpu.VMEM((8, 128), F32),
            pltpu.VMEM((depth, width + EXT), F32),
        ],
        compiler_params=pltpu.CompilerParams(vmem_limit_bytes=VMEM_LIMIT),
        name="local_state",
    )(forget, inputs, keys, values)


def prefix_states(slices_ref, out_ref, *, count, each):
    wide = out_ref.shape[1]
    width = wide - EXT
    level = jnp.full((each, 1), FLOOR_LOG, F32)
    state = jnp.zeros((each, width), F32)
    vector = jnp.zeros((each, 1), F32)
    per = 16 // each
    for group in range(count // per):
        block = slices_ref[group * 16 : (group + 1) * 16, :].astype(F32)
        starts = []
        for number in range(per):
            mine = block[number * each : (number + 1) * each]

            def column(first, how_many):
                return sum(mine[:, width + first + n : width + first + n + 1] for n in range(how_many))

            hi, lo, _ = pieces(vector)
            starts.append(
                jnp.concatenate([state, lay_columns(each, (hi, lo) + pieces(level))], axis=1)
            )
            shifted = level + column(5, 3)
            later = column(2, 3)
            level = jnp.maximum(shifted, later)
            old, new = jnp.exp(shifted - level), jnp.exp(later - level)
            state = old * state + new * mine[:, :width]
            vector = old * vector + new * column(0, 2)
        out_ref[group * 16 : (group + 1) * 16, :] = jnp.concatenate(starts, axis=0).astype(BF)


def run_prefix(slices, count):
    rows, wide = slices.shape
    return pl.pallas_call(
        functools.partial(prefix_states, count=count, each=rows // count),
        out_shape=jax.ShapeDtypeStruct((rows, wide), BF),
        name="prefix_states",
    )(slices)


def local_outputs(gates_ref, query_ref, key_ref, value_ref, numer_ref, stats_ref, state_ref):
    width = value_ref.shape[1]

    @pl.when(pl.program_id(0) == 0)
    def _():
        state_ref[...] = jnp.zeros_like(state_ref)

    per = query_ref.shape[0] // L
    scale = 1.0 / query_ref.shape[1] ** 0.5
    causal = lax.broadcasted_iota(jnp.int32, (L, L), 0) >= lax.broadcasted_iota(jnp.int32, (L, L), 1)
    ones = ones_column(L)
    for part in range(per):
        span = slice(part * L, (part + 1) * L)
        gates = jnp.concatenate(
            [gates_ref[part * 16 + half * 8 : part * 16 + half * 8 + 8, :] for half in range(2)], axis=1
        )
        columns = gates.T
        query, key, value = query_ref[span, :], key_ref[span, :], value_ref[span, :]
        key_t = key.T
        scores = dot(query, key_t) * scale
        probs = jnp.where(causal, jnp.exp(columns[:, 0:1] + gates[2:3, :]) * scores, 0.0)
        far = columns[:, 1:2] * scale
        state = state_ref[...]
        high = state.astype(BF)
        low = (state - high.astype(F32)).astype(BF)
        carried = dot(query, high) + dot(query, low)
        numer_ref[span, :] = dot(probs.astype(BF), value) + far * carried[:, :width]
        denom = jnp.sum(probs, axis=1, keepdims=True) + far * carried[:, width : width + 1]
        stats_ref[span, :] = lay_columns(L, (denom, columns[:, 4:5], columns[:, 5:6]))
        weighted = (key_t.astype(F32) * gates[3:4, :]).astype(BF)
        old = gates[6:7, 0:1]
        state_ref[:, :width] = old * state[:, :width] + dot(weighted, value)
        state_ref[:, width:] = old * state[:, width:] + dot(weighted, ones)


def run_local_outputs(gates, queries, keys, values):
    tokens, depth = keys.shape
    width = values.shape[1]
    block = 512
    return pl.pallas_call(
        local_outputs,
        grid=(tokens // block,),
        in_specs=[
            pl.BlockSpec((block // L * 16, 128), lambda i: (i, 0)),
            pl.BlockSpec((block, depth), lambda i: (i, 0)),
            pl.BlockSpec((block, depth), lambda i: (i, 0)),
            pl.BlockSpec((block, width), lambda i: (i, 0)),
        ],
        out_specs=[
            pl.BlockSpec((block, width), lambda i: (i, 0)),
            pl.BlockSpec((block, EXT), lambda i: (i, 0)),
        ],
        out_shape=[
            jax.ShapeDtypeStruct((tokens, width), F32),
            jax.ShapeDtypeStruct((tokens, EXT), F32),
        ],
        scratch_shapes=[pltpu.VMEM((depth, width + EXT), F32)],
        compiler_params=pltpu.CompilerParams(vmem_limit_bytes=VMEM_LIMIT),
        name="local_outputs",
    )(gates, queries, keys, values)


def finish(place_ref, query_ref, numer_ref, stats_ref, packet_ref, hidden_ref):
    width = numer_ref.shape[1]
    scale = 1.0 / query_ref.shape[1] ** 0.5
    ends = packet_ref[0:16, width:].astype(F32)[0:1]
    entering = ends[:, 2:3] + ends[:, 3:4] + ends[:, 4:5]
    stats = stats_ref[...]
    carry = stats[:, 1:2] + entering
    level = jnp.maximum(stats[:, 2:3], carry)
    own = jnp.exp(stats[:, 2:3] - level)
    far = jnp.exp(carry - level) * scale
    reach = dot(query_ref[...], packet_ref[...])
    denom = own * stats[:, 0:1] + far * (reach[:, width : width + 1] + reach[:, width + 1 : width + 2])
    share = 1.0 / jnp.maximum(jnp.abs(denom), 1.0)
    hidden_ref[...] = ((own * numer_ref[...] + far * reach[:, :width]) * share).astype(BF)


def run_finish(place, queries, numer, stats, packet, owners):
    tokens, depth = queries.shape
    width = numer.shape[1]
    rows = tokens // owners

    def pick(i, place):
        return (place[0], 0)

    return pl.pallas_call(
        finish,
        grid_spec=pltpu.PrefetchScalarGridSpec(
            num_scalar_prefetch=1,
            grid=(1,),
            in_specs=[
                pl.BlockSpec((rows, depth), pick),
                pl.BlockSpec((rows, width), pick),
                pl.BlockSpec((rows, EXT), pick),
                pl.BlockSpec(packet.shape, lambda i, place: (0, 0)),
            ],
            out_specs=pl.BlockSpec((rows, width), lambda i, place: (0, 0)),
        ),
        out_shape=jax.ShapeDtypeStruct((rows, width), BF),
        compiler_params=pltpu.CompilerParams(vmem_limit_bytes=VMEM_LIMIT),
        cost_estimate=pl.CostEstimate(
            flops=2 * rows * depth * packet.shape[1],
            bytes_accessed=rows * (2 * depth + 6 * width + 512),
            transcendentals=0,
        ),
        name="finish",
    )(place, queries, numer, stats, packet)


def norm(place_ref, gain_ref, *refs):
    out_ref = refs[-1]
    parts = refs[:-1]
    count = len(parts)
    width = parts[0].shape[1]
    square = jnp.zeros((parts[0].shape[0], 128), F32)
    for part in parts:
        wide = part[...].astype(F32)
        wide = wide * wide
        for piece in range(width // 128):
            square = square + wide[:, piece * 128 : (piece + 1) * 128]
    mean = jnp.sum(square, axis=1, keepdims=True) / (count * width)
    factor = lax.rsqrt(mean + EPSILON)
    for hop, part in enumerate(parts):
        head = lax.rem(place_ref[0] - hop + count, count)
        columns = pl.ds(pl.multiple_of(head * width, width), width)
        out_ref[:, columns] = (part[...].astype(F32) * factor * gain_ref[:, columns]).astype(BF)


def run_norm(place, gain, parts):
    rows, width = parts[0].shape
    block = 128
    total = width * len(parts)
    return pl.pallas_call(
        norm,
        grid_spec=pltpu.PrefetchScalarGridSpec(
            num_scalar_prefetch=1,
            grid=(rows // block,),
            in_specs=[pl.BlockSpec((1, total), lambda i, place: (0, 0))]
            + [pl.BlockSpec((block, width), lambda i, place: (i, 0))] * len(parts),
            out_specs=pl.BlockSpec((block, total), lambda i, place: (i, 0)),
        ),
        out_shape=jax.ShapeDtypeStruct((rows, total), BF),
        compiler_params=pltpu.CompilerParams(vmem_limit_bytes=VMEM_LIMIT),
        name="norm",
    )(place, gain, *parts)


def swap_slices(packet, count):
    rows, wide = packet.shape
    cut = packet.reshape(count, rows // count, wide)
    return lax.all_to_all(cut, "seq", 0, 0, tiled=True).reshape(rows, wide)


def shards(queries, key_vectors, value_vectors, input_gate, forget_gate, norm_gain):
    tokens = queries.shape[0]
    queries, keys, values = (a.reshape(tokens, a.shape[2]) for a in (queries, key_vectors, value_vectors))
    forget = forget_gate.reshape(tokens // 128, 128)
    inputs = input_gate.reshape(tokens // 128, 128)
    count = lax.axis_size("seq")
    owners = lax.axis_size("head")
    mine = lax.axis_index("head").astype(jnp.int32).reshape(1)
    packet, gates = run_local_state(forget, inputs, keys, values)
    slices = swap_slices(packet, count)
    numer, stats = run_local_outputs(gates, queries, keys, values)
    entering = swap_slices(run_prefix(slices, count), count)
    parts = [None] * owners
    for hop in (4, 3, 5, 2, 6, 1, 7, 0):
        hidden = run_finish(lax.rem(mine + hop, owners), queries, numer, stats, entering, owners)
        if hop:
            hidden = lax.ppermute(hidden, "head", [(i, (i + hop) % owners) for i in range(owners)])
        parts[hop] = hidden
    return run_norm(mine, norm_gain.reshape(1, -1), parts)


def solution(mesh):
    in_specs = (
        P("seq", "head", None),
        P("seq", "head", None),
        P("seq", "head", None),
        P("head", "seq"),
        P("head", "seq"),
        P(),
    )
    out_specs = P(("seq", "head"), None)
    return jax.shard_map(shards, mesh=mesh, in_specs=in_specs, out_specs=out_specs, check_vma=False)
```

```python
import functools

import jax
import jax.numpy as jnp
from jax import lax
from jax.experimental import pallas as pl
from jax.experimental.pallas import tpu as pltpu
from jax.sharding import PartitionSpec as P

EPSILON = 1e-06
FLOOR_LOG = -1e30
L = 256
EXT = 128
BLOCKS = 4
BF = jnp.bfloat16
F32 = jnp.float32
VMEM_LIMIT = 60 * 1024 * 1024
OUTPUTS_LIMIT = 60 * 1024 * 1024
SMALL_LIMIT = 20 * 1024 * 1024
FINISH_LIMIT = 24 * 1024 * 1024
HOPS = ((4, 3), (5, 2, 6, 1, 7, 0))


def dot(a, b):
    return jnp.dot(a, b, preferred_element_type=F32)


def pieces(x):
    hi = x.astype(BF).astype(F32)
    rest = x - hi
    mid = rest.astype(BF).astype(F32)
    return hi, mid, rest - mid


def ones_column(rows):
    return jnp.where(lax.broadcasted_iota(jnp.int32, (rows, EXT), 1) == 0, 1.0, 0.0).astype(BF)


def lay_columns(rows, columns):
    lane = lax.broadcasted_iota(jnp.int32, (rows, EXT), 1)
    out = jnp.zeros((rows, EXT), F32)
    for number, column in enumerate(columns):
        out = jnp.where(lane == number, column, out)
    return out


def gate_rows(forget_ref, input_ref, gates_ref, weight_ref, ends_ref):
    chunks = forget_ref.shape[0] * 128 // L

    def rows(ref):
        return jnp.concatenate(
            [ref[pl.ds(0, chunks, stride=2), :], ref[pl.ds(1, chunks, stride=2), :]], axis=1
        )

    forget = rows(forget_ref)
    lgate = jnp.minimum(forget, 0.0) - jnp.log1p(jnp.exp(-jnp.abs(forget)))
    lane = lax.broadcasted_iota(jnp.int32, (chunks, L), 1)
    within = lgate
    shift = 1
    while shift < L:
        within = within + jnp.where(lane >= shift, pltpu.roll(within, shift, 1), 0.0)
        shift *= 2
    lead = rows(input_ref) - within
    top = lead
    shift = 1
    while shift < L:
        top = jnp.maximum(top, jnp.where(lane >= shift, pltpu.roll(top, shift, 1), -jnp.inf))
        shift *= 2
    total = within[:, L - 1 :]
    chunk_top = total + top[:, L - 1 :]
    row = lax.broadcasted_iota(jnp.int32, (chunks, 1), 0)
    level = jnp.full((1, 1), FLOOR_LOG, F32)
    before = jnp.zeros((1, 1), F32)
    enter = jnp.zeros((chunks, 1), F32)
    leave = jnp.zeros((chunks, 1), F32)
    prefix = jnp.zeros((chunks, 1), F32)
    for c in range(chunks):
        enter = jnp.where(row == c, level, enter)
        prefix = jnp.where(row == c, before, prefix)
        level = jnp.maximum(level + total[c : c + 1], chunk_top[c : c + 1])
        before = before + total[c : c + 1]
        leave = jnp.where(row == c, level, leave)
    after = jnp.zeros((1, 1), F32)
    suffix = jnp.zeros((chunks, 1), F32)
    for c in reversed(range(chunks)):
        suffix = jnp.where(row == c, after, suffix)
        after = after + total[c : c + 1]
    carry = within + enter
    levels = jnp.maximum(within + top, carry)
    keylog = lead + total
    weight_ref[...] = jnp.exp(keylog + suffix - level)
    ends_ref[0:1, :] = jnp.broadcast_to(level, (1, 128))
    ends_ref[1:2, :] = jnp.broadcast_to(before, (1, 128))

    def put(number, value):
        for half in range(2):
            gates_ref[pl.ds(half * 8 + number, chunks, stride=16), :] = value[:, half * 128 : (half + 1) * 128]

    put(0, within - levels)
    put(1, jnp.exp(carry - levels))
    put(2, lead)
    put(3, jnp.exp(keylog - leave))
    put(4, within + prefix)
    put(5, levels)
    put(6, jnp.broadcast_to(jnp.exp(enter + total - leave), (chunks, L)))
    put(7, jnp.zeros((chunks, L), F32))


def fetch(pairs, sems):
    waits = []
    for row, blocks in enumerate(pairs):
        started = []
        for column, (source, target) in enumerate(blocks):
            copy = pltpu.make_async_copy(source, target, sems.at[row, column])
            copy.start()
            started.append(copy)
        waits.append(started)
    return waits


def local_state(
    forget_ref, input_ref, key_hbm, value_hbm, packet_ref, gates_ref, key_ref, value_ref, weight_ref, ends_ref, sems
):
    tokens, rows = key_ref.shape
    width = value_ref.shape[1]
    block = tokens // sems.shape[0]
    spans = [pl.ds(number * block, block) for number in range(sems.shape[0])]
    waits = fetch(
        [
            [(key_hbm.at[span, :], key_ref.at[span, :]), (value_hbm.at[span, :], value_ref.at[span, :])]
            for span in spans
        ],
        sems,
    )
    gate_rows(forget_ref, input_ref, gates_ref, weight_ref, ends_ref)
    ones = ones_column(block)
    per = block // L
    matrix = vector = None
    for number, span in enumerate(spans):
        for copy in waits[number]:
            copy.wait()
        weight = jnp.concatenate(
            [weight_ref[number * per + part : number * per + part + 1, :] for part in range(per)], axis=1
        )
        weighted = (key_ref[span, :].T.astype(F32) * weight).astype(BF)
        add_matrix, add_vector = dot(weighted, value_ref[span, :]), dot(weighted, ones)
        matrix = add_matrix if matrix is None else matrix + add_matrix
        vector = add_vector if vector is None else vector + add_vector
    packet_ref[:, :width] = matrix.astype(BF)
    level = pieces(ends_ref[0:1, 0:1])
    decay = pieces(ends_ref[1:2, 0:1])
    packet_ref[:, width:] = lay_columns(rows, pieces(vector[:, 0:1])[:2] + level + decay).astype(BF)


def run_local_state(forget, inputs, keys, values):
    tokens, depth = keys.shape
    width = values.shape[1]
    chunks = tokens // L
    vmem = pl.BlockSpec(memory_space=pltpu.VMEM)
    hbm = pl.BlockSpec(memory_space=pl.ANY)
    return pl.pallas_call(
        local_state,
        in_specs=[vmem, vmem, hbm, hbm],
        out_specs=[vmem, vmem],
        out_shape=[
            jax.ShapeDtypeStruct((depth, width + EXT), BF),
            jax.ShapeDtypeStruct((chunks * 16, 128), F32),
        ],
        scratch_shapes=[
            pltpu.VMEM((tokens, depth), BF),
            pltpu.VMEM((tokens, width), BF),
            pltpu.VMEM((chunks, L), F32),
            pltpu.VMEM((8, 128), F32),
            pltpu.SemaphoreType.DMA((BLOCKS, 2)),
        ],
        compiler_params=pltpu.CompilerParams(vmem_limit_bytes=VMEM_LIMIT),
        name="local_state",
    )(forget, inputs, keys, values)


def prefix_states(slices_ref, out_ref, *, count, each):
    wide = out_ref.shape[1]
    width = wide - EXT
    level = jnp.full((each, 1), FLOOR_LOG, F32)
    state = jnp.zeros((each, width), F32)
    vector = jnp.zeros((each, 1), F32)
    per = 16 // each
    for group in range(count // per):
        block = slices_ref[group * 16 : (group + 1) * 16, :].astype(F32)
        starts = []
        for number in range(per):
            mine = block[number * each : (number + 1) * each]

            def column(first, how_many):
                return sum(mine[:, width + first + n : width + first + n + 1] for n in range(how_many))

            hi, lo, _ = pieces(vector)
            starts.append(
                jnp.concatenate([state, lay_columns(each, (hi, lo) + pieces(level))], axis=1)
            )
            shifted = level + column(5, 3)
            later = column(2, 3)
            level = jnp.maximum(shifted, later)
            old, new = jnp.exp(shifted - level), jnp.exp(later - level)
            state = old * state + new * mine[:, :width]
            vector = old * vector + new * column(0, 2)
        out_ref[group * 16 : (group + 1) * 16, :] = jnp.concatenate(starts, axis=0).astype(BF)


def run_prefix(slices, count):
    rows, wide = slices.shape
    return pl.pallas_call(
        functools.partial(prefix_states, count=count, each=rows // count),
        out_shape=jax.ShapeDtypeStruct((rows, wide), BF),
        compiler_params=pltpu.CompilerParams(vmem_limit_bytes=SMALL_LIMIT),
        name="prefix_states",
    )(slices)


def local_outputs(gates_ref, query_ref, key_ref, value_ref, *refs):
    start_ref = refs[-4] if len(refs) == 6 else None
    numer_ref, stats_ref, state_ref = refs[-3:]
    width = value_ref.shape[1]

    @pl.when(pl.program_id(0) == 0)
    def _():
        state_ref[...] = jnp.zeros_like(state_ref) if start_ref is None else start_ref[...]

    per = query_ref.shape[0] // L
    scale = 1.0 / query_ref.shape[1] ** 0.5
    causal = lax.broadcasted_iota(jnp.int32, (L, L), 0) >= lax.broadcasted_iota(jnp.int32, (L, L), 1)
    ones = ones_column(L)
    for part in range(per):
        span = slice(part * L, (part + 1) * L)
        gates = jnp.concatenate(
            [gates_ref[part * 16 + half * 8 : part * 16 + half * 8 + 8, :] for half in range(2)], axis=1
        )
        columns = gates.T
        query, key, value = query_ref[span, :], key_ref[span, :], value_ref[span, :]
        key_t = key.T
        scores = dot(query, key_t) * scale
        probs = jnp.where(causal, jnp.exp(columns[:, 0:1] + gates[2:3, :]) * scores, 0.0)
        far = columns[:, 1:2] * scale
        state = state_ref[...]
        high = state.astype(BF)
        low = (state - high.astype(F32)).astype(BF)
        carried = dot(query, high) + dot(query, low)
        numer_ref[span, :] = (dot(probs.astype(BF), value) + far * carried[:, :width]).astype(BF)
        denom = jnp.sum(probs, axis=1, keepdims=True) + far * carried[:, width : width + 1]
        flat = lay_columns(L, (denom,)).T[:8]
        for half in range(2):
            first = part * 16 + half * 8
            stats_ref[first : first + 8, :] = flat[:, half * 128 : (half + 1) * 128]
        weighted = (key_t.astype(F32) * gates[3:4, :]).astype(BF)
        old = gates[6:7, 0:1]
        state_ref[:, :width] = old * state[:, :width] + dot(weighted, value)
        state_ref[:, width:] = old * state[:, width:] + dot(weighted, ones)


def run_local_outputs(gates, queries, keys, values, half, before=None):
    tokens, depth = keys.shape
    width = values.shape[1]
    block = 1024
    steps = tokens // block // 2
    first = half * steps

    def at(i):
        return (first + i, 0)

    whole = pl.BlockSpec((depth, width + EXT), lambda i: (0, 0))
    return pl.pallas_call(
        local_outputs,
        grid=(steps,),
        in_specs=[
            pl.BlockSpec((block // L * 16, 128), at),
            pl.BlockSpec((block, depth), at),
            pl.BlockSpec((block, depth), at),
            pl.BlockSpec((block, width), at),
        ]
        + ([pl.BlockSpec(memory_space=pl.ANY)] * 2 + [whole] if half else []),
        out_specs=[
            pl.BlockSpec((block, width), at),
            pl.BlockSpec((block // L * 16, 128), at),
            whole,
        ],
        out_shape=[
            jax.ShapeDtypeStruct((tokens, width), BF),
            jax.ShapeDtypeStruct((tokens // L * 16, 128), F32),
            jax.ShapeDtypeStruct((depth, width + EXT), F32),
        ],
        input_output_aliases={4: 0, 5: 1} if half else {},
        compiler_params=pltpu.CompilerParams(vmem_limit_bytes=OUTPUTS_LIMIT),
        name="local_outputs",
    )(gates, queries, keys, values, *(before or ()))


def finish(
    place_ref, query_hbm, numer_hbm, gates_ref, stats_ref, packet_ref, *refs, hops, owners
):
    outs = refs[: len(hops)]
    query_ref, numer_ref, hidden_ref, in_sems, out_sems = refs[len(hops) :]
    rows = query_ref.shape[1]
    width = numer_ref.shape[2]
    scale = 1.0 / query_ref.shape[2] ** 0.5
    targets = [lax.rem(place_ref[0] + hop, owners) for hop in hops]
    blocks = []
    for number, target in enumerate(targets):
        span = pl.ds(pl.multiple_of(target * rows, rows), rows)
        blocks.append(
            [(query_hbm.at[span, :], query_ref.at[number]), (numer_hbm.at[span, :], numer_ref.at[number])]
        )
    waits = fetch(blocks, in_sems)
    ends = packet_ref[0:16, width:].astype(F32)[0:1]
    entering = ends[:, 2:3] + ends[:, 3:4] + ends[:, 4:5]
    copies = []
    for number, target in enumerate(targets):
        for copy in waits[number]:
            copy.wait()
        tall = rows // L * 16
        tile = pl.ds(pl.multiple_of(target * tall, tall), tall)
        gates, stats = gates_ref[tile, :], stats_ref[tile, :]
        row = lax.broadcasted_iota(jnp.int32, (8, L), 0)
        for part in range(rows // L):
            span = slice(part * L, (part + 1) * L)

            def rows_of(array):
                first = part * 16
                return jnp.concatenate([array[first : first + 8], array[first + 8 : first + 16]], axis=1)

            marks, sums = rows_of(gates), rows_of(stats)
            local = marks[5:6]
            carry = marks[4:5] + entering
            level = jnp.maximum(local, carry)
            own = jnp.exp(local - level)
            far = jnp.exp(carry - level) * scale
            columns = jnp.where(row == 0, own, jnp.where(row == 1, far, own * sums[0:1])).T
            own, far = columns[:, 0:1], columns[:, 1:2]
            reach = dot(query_ref[number, span, :], packet_ref[...])
            vector = reach[:, width : width + 1] + reach[:, width + 1 : width + 2]
            share = 1.0 / jnp.maximum(jnp.abs(columns[:, 2:3] + far * vector), 1.0)
            hidden_ref[number, span, :] = (
                (own * share) * numer_ref[number, span, :].astype(F32) + (far * share) * reach[:, :width]
            ).astype(BF)
        copy = pltpu.make_async_copy(hidden_ref.at[number], outs[number], out_sems.at[number])
        copy.start()
        copies.append(copy)
    for copy in copies:
        copy.wait()


def run_finish(place, queries, numer, gates, stats, packet, owners, hops):
    tokens, depth = queries.shape
    width = numer.shape[1]
    rows = tokens // owners
    count = len(hops)
    vmem = pl.BlockSpec(memory_space=pltpu.VMEM)
    hbm = pl.BlockSpec(memory_space=pltpu.HBM)
    anywhere = pl.BlockSpec(memory_space=pl.ANY)
    return pl.pallas_call(
        functools.partial(finish, hops=hops, owners=owners),
        in_specs=[pl.BlockSpec(memory_space=pltpu.SMEM), hbm, hbm, vmem, vmem, vmem],
        out_specs=[anywhere] * count,
        out_shape=[jax.ShapeDtypeStruct((rows, width), BF)] * count,
        scratch_shapes=[
            pltpu.VMEM((count, rows, depth), BF),
            pltpu.VMEM((count, rows, width), BF),
            pltpu.VMEM((count, rows, width), BF),
            pltpu.SemaphoreType.DMA((count, 2)),
            pltpu.SemaphoreType.DMA((count,)),
        ],
        compiler_params=pltpu.CompilerParams(vmem_limit_bytes=FINISH_LIMIT),
        cost_estimate=pl.CostEstimate(
            flops=2 * count * rows * depth * packet.shape[1],
            bytes_accessed=count * rows * (2 * depth + 4 * width),
            transcendentals=0,
        ),
        name="finish",
    )(place, queries, numer, gates, stats, packet)


def norm(place_ref, gain_ref, *refs):
    out_ref = refs[-1]
    parts = refs[:-1]
    count = len(parts)
    width = parts[0].shape[1]
    square = jnp.zeros((parts[0].shape[0], 128), F32)
    for part in parts:
        wide = part[...].astype(F32)
        wide = wide * wide
        for piece in range(width // 128):
            square = square + wide[:, piece * 128 : (piece + 1) * 128]
    mean = jnp.sum(square, axis=1, keepdims=True) / (count * width)
    factor = lax.rsqrt(mean + EPSILON)
    for hop, part in enumerate(parts):
        head = lax.rem(place_ref[0] - hop + count, count)
        columns = pl.ds(pl.multiple_of(head * width, width), width)
        out_ref[:, columns] = (part[...].astype(F32) * factor * gain_ref[:, columns]).astype(BF)


def run_norm(place, gain, parts):
    rows, width = parts[0].shape
    block = 128
    total = width * len(parts)
    return pl.pallas_call(
        norm,
        grid_spec=pltpu.PrefetchScalarGridSpec(
            num_scalar_prefetch=1,
            grid=(rows // block,),
            in_specs=[pl.BlockSpec((1, total), lambda i, place: (0, 0))]
            + [pl.BlockSpec((block, width), lambda i, place: (i, 0))] * len(parts),
            out_specs=pl.BlockSpec((block, total), lambda i, place: (i, 0)),
        ),
        out_shape=jax.ShapeDtypeStruct((rows, total), BF),
        compiler_params=pltpu.CompilerParams(vmem_limit_bytes=SMALL_LIMIT),
        name="norm",
    )(place, gain, *parts)


def swap_slices(packet, count):
    rows, wide = packet.shape
    cut = packet.reshape(count, rows // count, wide)
    return lax.all_to_all(cut, "seq", 0, 0, tiled=True).reshape(rows, wide)


def shards(queries, key_vectors, value_vectors, input_gate, forget_gate, norm_gain):
    tokens = queries.shape[0]
    queries, keys, values = (a.reshape(tokens, a.shape[2]) for a in (queries, key_vectors, value_vectors))
    forget = forget_gate.reshape(tokens // 128, 128)
    inputs = input_gate.reshape(tokens // 128, 128)
    count = lax.axis_size("seq")
    owners = lax.axis_size("head")
    mine = lax.axis_index("head").astype(jnp.int32).reshape(1)
    packet, gates = run_local_state(forget, inputs, keys, values)
    slices = swap_slices(packet, count)
    before = run_local_outputs(gates, queries, keys, values, 0)
    slices, before = lax.optimization_barrier((slices, before))
    starts = run_prefix(slices, count)
    starts, before = lax.optimization_barrier((starts, before))
    entering = swap_slices(starts, count)
    numer, stats, _ = run_local_outputs(gates, queries, keys, values, 1, before)
    parts = [None] * owners
    place = mine
    for hops in HOPS:
        group = run_finish(place, queries, numer, gates, stats, entering, owners, hops)
        for hop, hidden in zip(hops, group):
            if hop:
                hidden = lax.ppermute(hidden, "head", [(i, (i + hop) % owners) for i in range(owners)])
            parts[hop] = hidden
    return run_norm(mine, norm_gain.reshape(1, -1), parts)


def solution(mesh):
    in_specs = (
        P("seq", "head", None),
        P("seq", "head", None),
        P("seq", "head", None),
        P("head", "seq"),
        P("head", "seq"),
        P(),
    )
    out_specs = P(("seq", "head"), None)
    return jax.shard_map(shards, mesh=mesh, in_specs=in_specs, out_specs=out_specs, check_vma=False)
```

```python
import functools

import jax
import jax.numpy as jnp
from jax import lax
from jax.experimental import pallas as pl
from jax.experimental.pallas import tpu as pltpu
from jax.sharding import PartitionSpec as P

EPSILON = 1e-06
FLOOR_LOG = -1e30
L = 256
EXT = 128
BLOCKS = 4
BF = jnp.bfloat16
F32 = jnp.float32
VMEM_LIMIT = 60 * 1024 * 1024
OUTPUTS_LIMIT = 60 * 1024 * 1024
SMALL_LIMIT = 20 * 1024 * 1024
FINISH_LIMITS = (61 * 1024 * 1024, 61 * 1024 * 1024, 61 * 1024 * 1024,)
HOPS = ((4,), (3, 5), (2, 6, 1, 7, 0))


def dot(a, b):
    return jnp.dot(a, b, preferred_element_type=F32)


def pieces(x):
    hi = x.astype(BF).astype(F32)
    rest = x - hi
    mid = rest.astype(BF).astype(F32)
    return hi, mid, rest - mid


def ones_column(rows):
    return jnp.where(lax.broadcasted_iota(jnp.int32, (rows, EXT), 1) == 0, 1.0, 0.0).astype(BF)


def lay_columns(rows, columns):
    lane = lax.broadcasted_iota(jnp.int32, (rows, EXT), 1)
    out = jnp.zeros((rows, EXT), F32)
    for number, column in enumerate(columns):
        out = jnp.where(lane == number, column, out)
    return out


def gate_rows(forget_ref, input_ref, gates_ref, weight_ref, ends_ref):
    chunks = forget_ref.shape[0] * 128 // L

    def rows(ref):
        return jnp.concatenate(
            [ref[pl.ds(0, chunks, stride=2), :], ref[pl.ds(1, chunks, stride=2), :]], axis=1
        )

    forget = rows(forget_ref)
    lgate = jnp.minimum(forget, 0.0) - jnp.log1p(jnp.exp(-jnp.abs(forget)))
    lane = lax.broadcasted_iota(jnp.int32, (chunks, L), 1)
    within = lgate
    shift = 1
    while shift < L:
        within = within + jnp.where(lane >= shift, pltpu.roll(within, shift, 1), 0.0)
        shift *= 2
    lead = rows(input_ref) - within
    top = lead
    shift = 1
    while shift < L:
        top = jnp.maximum(top, jnp.where(lane >= shift, pltpu.roll(top, shift, 1), -jnp.inf))
        shift *= 2
    total = within[:, L - 1 :]
    chunk_top = total + top[:, L - 1 :]
    row = lax.broadcasted_iota(jnp.int32, (chunks, 1), 0)
    level = jnp.full((1, 1), FLOOR_LOG, F32)
    before = jnp.zeros((1, 1), F32)
    enter = jnp.zeros((chunks, 1), F32)
    leave = jnp.zeros((chunks, 1), F32)
    prefix = jnp.zeros((chunks, 1), F32)
    for c in range(chunks):
        enter = jnp.where(row == c, level, enter)
        prefix = jnp.where(row == c, before, prefix)
        level = jnp.maximum(level + total[c : c + 1], chunk_top[c : c + 1])
        before = before + total[c : c + 1]
        leave = jnp.where(row == c, level, leave)
    after = jnp.zeros((1, 1), F32)
    suffix = jnp.zeros((chunks, 1), F32)
    for c in reversed(range(chunks)):
        suffix = jnp.where(row == c, after, suffix)
        after = after + total[c : c + 1]
    carry = within + enter
    levels = jnp.maximum(within + top, carry)
    keylog = lead + total
    weight_ref[...] = jnp.exp(keylog + suffix - level)
    ends_ref[0:1, :] = jnp.broadcast_to(level, (1, 128))
    ends_ref[1:2, :] = jnp.broadcast_to(before, (1, 128))

    def put(number, value):
        for half in range(2):
            gates_ref[pl.ds(half * 8 + number, chunks, stride=16), :] = value[:, half * 128 : (half + 1) * 128]

    put(0, within - levels)
    put(1, jnp.exp(carry - levels))
    put(2, lead)
    put(3, jnp.exp(keylog - leave))
    put(4, within + prefix)
    put(5, levels)
    put(6, jnp.broadcast_to(jnp.exp(enter + total - leave), (chunks, L)))
    put(7, jnp.zeros((chunks, L), F32))


def fetch(pairs, sems):
    waits = []
    for row, blocks in enumerate(pairs):
        started = []
        for column, (source, target) in enumerate(blocks):
            copy = pltpu.make_async_copy(source, target, sems.at[row, column])
            copy.start()
            started.append(copy)
        waits.append(started)
    return waits


def local_state(
    forget_ref, input_ref, key_hbm, value_hbm, packet_ref, gates_ref, key_ref, value_ref, weight_ref, ends_ref, sems
):
    tokens, rows = key_ref.shape
    width = value_ref.shape[1]
    block = tokens // sems.shape[0]
    spans = [pl.ds(number * block, block) for number in range(sems.shape[0])]
    waits = fetch(
        [
            [(key_hbm.at[span, :], key_ref.at[span, :]), (value_hbm.at[span, :], value_ref.at[span, :])]
            for span in spans
        ],
        sems,
    )
    gate_rows(forget_ref, input_ref, gates_ref, weight_ref, ends_ref)
    ones = ones_column(block)
    per = block // L
    matrix = vector = None
    for number, span in enumerate(spans):
        for copy in waits[number]:
            copy.wait()
        weight = jnp.concatenate(
            [weight_ref[number * per + part : number * per + part + 1, :] for part in range(per)], axis=1
        )
        weighted = (key_ref[span, :].T.astype(F32) * weight).astype(BF)
        add_matrix, add_vector = dot(weighted, value_ref[span, :]), dot(weighted, ones)
        matrix = add_matrix if matrix is None else matrix + add_matrix
        vector = add_vector if vector is None else vector + add_vector
    packet_ref[:, :width] = matrix.astype(BF)
    level = pieces(ends_ref[0:1, 0:1])
    decay = pieces(ends_ref[1:2, 0:1])
    packet_ref[:, width:] = lay_columns(rows, pieces(vector[:, 0:1])[:2] + level + decay).astype(BF)


def run_local_state(forget, inputs, keys, values):
    tokens, depth = keys.shape
    width = values.shape[1]
    chunks = tokens // L
    vmem = pl.BlockSpec(memory_space=pltpu.VMEM)
    hbm = pl.BlockSpec(memory_space=pl.ANY)
    return pl.pallas_call(
        local_state,
        in_specs=[vmem, vmem, hbm, hbm],
        out_specs=[vmem, vmem],
        out_shape=[
            jax.ShapeDtypeStruct((depth, width + EXT), BF),
            jax.ShapeDtypeStruct((chunks * 16, 128), F32),
        ],
        scratch_shapes=[
            pltpu.VMEM((tokens, depth), BF),
            pltpu.VMEM((tokens, width), BF),
            pltpu.VMEM((chunks, L), F32),
            pltpu.VMEM((8, 128), F32),
            pltpu.SemaphoreType.DMA((BLOCKS, 2)),
        ],
        compiler_params=pltpu.CompilerParams(vmem_limit_bytes=VMEM_LIMIT),
        name="local_state",
    )(forget, inputs, keys, values)


def prefix_states(slices_ref, out_ref, *, count, each):
    wide = out_ref.shape[1]
    width = wide - EXT
    level = jnp.full((each, 1), FLOOR_LOG, F32)
    state = jnp.zeros((each, width), F32)
    vector = jnp.zeros((each, 1), F32)
    per = 16 // each
    for group in range(count // per):
        block = slices_ref[group * 16 : (group + 1) * 16, :].astype(F32)
        starts = []
        for number in range(per):
            mine = block[number * each : (number + 1) * each]

            def column(first, how_many):
                return sum(mine[:, width + first + n : width + first + n + 1] for n in range(how_many))

            hi, lo, _ = pieces(vector)
            starts.append(
                jnp.concatenate([state, lay_columns(each, (hi, lo) + pieces(level))], axis=1)
            )
            shifted = level + column(5, 3)
            later = column(2, 3)
            level = jnp.maximum(shifted, later)
            old, new = jnp.exp(shifted - level), jnp.exp(later - level)
            state = old * state + new * mine[:, :width]
            vector = old * vector + new * column(0, 2)
        out_ref[group * 16 : (group + 1) * 16, :] = jnp.concatenate(starts, axis=0).astype(BF)


def run_prefix(slices, count):
    rows, wide = slices.shape
    return pl.pallas_call(
        functools.partial(prefix_states, count=count, each=rows // count),
        out_shape=jax.ShapeDtypeStruct((rows, wide), BF),
        compiler_params=pltpu.CompilerParams(vmem_limit_bytes=SMALL_LIMIT),
        name="prefix_states",
    )(slices)


def local_outputs(gates_ref, query_ref, key_ref, value_ref, *refs):
    start_ref = refs[-4] if len(refs) == 6 else None
    numer_ref, stats_ref, state_ref = refs[-3:]
    width = value_ref.shape[1]

    @pl.when(pl.program_id(0) == 0)
    def _():
        state_ref[...] = jnp.zeros_like(state_ref) if start_ref is None else start_ref[...]

    per = query_ref.shape[0] // L
    scale = 1.0 / query_ref.shape[1] ** 0.5
    causal = lax.broadcasted_iota(jnp.int32, (L, L), 0) >= lax.broadcasted_iota(jnp.int32, (L, L), 1)
    ones = ones_column(L)
    for part in range(per):
        span = slice(part * L, (part + 1) * L)
        gates = jnp.concatenate(
            [gates_ref[part * 16 + half * 8 : part * 16 + half * 8 + 8, :] for half in range(2)], axis=1
        )
        columns = gates.T
        query, key, value = query_ref[span, :], key_ref[span, :], value_ref[span, :]
        key_t = key.T
        scores = dot(query, key_t) * scale
        probs = jnp.where(causal, jnp.exp(columns[:, 0:1] + gates[2:3, :]) * scores, 0.0)
        far = columns[:, 1:2] * scale
        state = state_ref[...]
        high = state.astype(BF)
        low = (state - high.astype(F32)).astype(BF)
        carried = dot(query, high) + dot(query, low)
        numer_ref[span, :] = (dot(probs.astype(BF), value) + far * carried[:, :width]).astype(BF)
        denom = jnp.sum(probs, axis=1, keepdims=True) + far * carried[:, width : width + 1]
        flat = lay_columns(L, (denom,)).T[:8]
        for half in range(2):
            first = part * 16 + half * 8
            stats_ref[first : first + 8, :] = flat[:, half * 128 : (half + 1) * 128]
        weighted = (key_t.astype(F32) * gates[3:4, :]).astype(BF)
        old = gates[6:7, 0:1]
        state_ref[:, :width] = old * state[:, :width] + dot(weighted, value)
        state_ref[:, width:] = old * state[:, width:] + dot(weighted, ones)


def run_local_outputs(gates, queries, keys, values, half, before=None):
    tokens, depth = keys.shape
    width = values.shape[1]
    block = 1024
    steps = tokens // block // 2
    first = half * steps

    def at(i):
        return (first + i, 0)

    whole = pl.BlockSpec((depth, width + EXT), lambda i: (0, 0))
    return pl.pallas_call(
        local_outputs,
        grid=(steps,),
        in_specs=[
            pl.BlockSpec((block // L * 16, 128), at),
            pl.BlockSpec((block, depth), at),
            pl.BlockSpec((block, depth), at),
            pl.BlockSpec((block, width), at),
        ]
        + ([pl.BlockSpec(memory_space=pl.ANY)] * 2 + [whole] if half else []),
        out_specs=[
            pl.BlockSpec((block, width), at),
            pl.BlockSpec((block // L * 16, 128), at),
            whole,
        ],
        out_shape=[
            jax.ShapeDtypeStruct((tokens, width), BF),
            jax.ShapeDtypeStruct((tokens // L * 16, 128), F32),
            jax.ShapeDtypeStruct((depth, width + EXT), F32),
        ],
        input_output_aliases={4: 0, 5: 1} if half else {},
        compiler_params=pltpu.CompilerParams(vmem_limit_bytes=OUTPUTS_LIMIT),
        name="local_outputs",
    )(gates, queries, keys, values, *(before or ()))


def finish(
    place_ref, query_hbm, numer_hbm, gates_hbm, stats_hbm, packet_hbm, *refs, hops, owners
):
    outs = refs[: len(hops)]
    query_ref, numer_ref, gates_ref, stats_ref, packet_ref, hidden_ref, in_sems, all_sems, out_sems = refs[len(hops) :]
    first = fetch([[(packet_hbm, packet_ref), (gates_hbm, gates_ref), (stats_hbm, stats_ref)]], all_sems)[0]
    rows = query_ref.shape[1]
    width = numer_ref.shape[2]
    scale = 1.0 / query_ref.shape[2] ** 0.5
    targets = [lax.rem(place_ref[0] + hop, owners) for hop in hops]
    blocks = []
    for number, target in enumerate(targets):
        span = pl.ds(pl.multiple_of(target * rows, rows), rows)
        blocks.append(
            [(query_hbm.at[span, :], query_ref.at[number]), (numer_hbm.at[span, :], numer_ref.at[number])]
        )
    waits = fetch(blocks, in_sems)
    for copy in first:
        copy.wait()
    ends = packet_ref[0:16, width:].astype(F32)[0:1]
    entering = ends[:, 2:3] + ends[:, 3:4] + ends[:, 4:5]
    copies = []
    for number, target in enumerate(targets):
        for copy in waits[number]:
            copy.wait()
        tall = rows // L * 16
        tile = pl.ds(pl.multiple_of(target * tall, tall), tall)
        gates, stats = gates_ref[tile, :], stats_ref[tile, :]
        row = lax.broadcasted_iota(jnp.int32, (8, L), 0)
        for part in range(rows // L):
            span = slice(part * L, (part + 1) * L)

            def rows_of(array):
                first = part * 16
                return jnp.concatenate([array[first : first + 8], array[first + 8 : first + 16]], axis=1)

            marks, sums = rows_of(gates), rows_of(stats)
            local = marks[5:6]
            carry = marks[4:5] + entering
            level = jnp.maximum(local, carry)
            own = jnp.exp(local - level)
            far = jnp.exp(carry - level) * scale
            columns = jnp.where(row == 0, own, jnp.where(row == 1, far, own * sums[0:1])).T
            own, far = columns[:, 0:1], columns[:, 1:2]
            reach = dot(query_ref[number, span, :], packet_ref[...])
            vector = reach[:, width : width + 1] + reach[:, width + 1 : width + 2]
            share = 1.0 / jnp.maximum(jnp.abs(columns[:, 2:3] + far * vector), 1.0)
            hidden_ref[number, span, :] = (
                (own * share) * numer_ref[number, span, :].astype(F32) + (far * share) * reach[:, :width]
            ).astype(BF)
        copy = pltpu.make_async_copy(hidden_ref.at[number], outs[number], out_sems.at[number])
        copy.start()
        copies.append(copy)
    for copy in copies:
        copy.wait()


def run_finish(place, queries, numer, gates, stats, packet, owners, hops, limit):
    tokens, depth = queries.shape
    width = numer.shape[1]
    rows = tokens // owners
    count = len(hops)
    anywhere = pl.BlockSpec(memory_space=pl.ANY)
    return pl.pallas_call(
        functools.partial(finish, hops=hops, owners=owners),
        in_specs=[pl.BlockSpec(memory_space=pltpu.SMEM)] + [anywhere] * 5,
        out_specs=[anywhere] * count,
        out_shape=[jax.ShapeDtypeStruct((rows, width), BF)] * count,
        scratch_shapes=[
            pltpu.VMEM((count, rows, depth), BF),
            pltpu.VMEM((count, rows, width), BF),
            pltpu.VMEM(gates.shape, F32),
            pltpu.VMEM(stats.shape, F32),
            pltpu.VMEM(packet.shape, BF),
            pltpu.VMEM((count, rows, width), BF),
            pltpu.SemaphoreType.DMA((count, 2)),
            pltpu.SemaphoreType.DMA((1, 3)),
            pltpu.SemaphoreType.DMA((count,)),
        ],
        compiler_params=pltpu.CompilerParams(vmem_limit_bytes=limit),
        cost_estimate=pl.CostEstimate(
            flops=2 * count * rows * depth * packet.shape[1],
            bytes_accessed=count * rows * (2 * depth + 4 * width),
            transcendentals=0,
        ),
        name="finish",
    )(place, queries, numer, gates, stats, packet)


def norm(place_ref, gain_ref, *refs):
    out_ref = refs[-1]
    parts = refs[:-1]
    count = len(parts)
    width = parts[0].shape[1]
    square = jnp.zeros((parts[0].shape[0], 128), F32)
    for part in parts:
        wide = part[...].astype(F32)
        wide = wide * wide
        for piece in range(width // 128):
            square = square + wide[:, piece * 128 : (piece + 1) * 128]
    mean = jnp.sum(square, axis=1, keepdims=True) / (count * width)
    factor = lax.rsqrt(mean + EPSILON)
    for hop, part in enumerate(parts):
        head = lax.rem(place_ref[0] - hop + count, count)
        columns = pl.ds(pl.multiple_of(head * width, width), width)
        out_ref[:, columns] = (part[...].astype(F32) * factor * gain_ref[:, columns]).astype(BF)


def run_norm(place, gain, parts):
    rows, width = parts[0].shape
    block = 128
    total = width * len(parts)
    return pl.pallas_call(
        norm,
        grid_spec=pltpu.PrefetchScalarGridSpec(
            num_scalar_prefetch=1,
            grid=(rows // block,),
            in_specs=[pl.BlockSpec((1, total), lambda i, place: (0, 0))]
            + [pl.BlockSpec((block, width), lambda i, place: (i, 0))] * len(parts),
            out_specs=pl.BlockSpec((block, total), lambda i, place: (i, 0)),
        ),
        out_shape=jax.ShapeDtypeStruct((rows, total), BF),
        compiler_params=pltpu.CompilerParams(vmem_limit_bytes=SMALL_LIMIT),
        name="norm",
    )(place, gain, *parts)


def swap_slices(packet, count):
    rows, wide = packet.shape
    cut = packet.reshape(count, rows // count, wide)
    return lax.all_to_all(cut, "seq", 0, 0, tiled=True).reshape(rows, wide)


def shards(queries, key_vectors, value_vectors, input_gate, forget_gate, norm_gain):
    tokens = queries.shape[0]
    queries, keys, values = (a.reshape(tokens, a.shape[2]) for a in (queries, key_vectors, value_vectors))
    forget = forget_gate.reshape(tokens // 128, 128)
    inputs = input_gate.reshape(tokens // 128, 128)
    count = lax.axis_size("seq")
    owners = lax.axis_size("head")
    mine = lax.axis_index("head").astype(jnp.int32).reshape(1)
    packet, gates = run_local_state(forget, inputs, keys, values)
    slices = swap_slices(packet, count)
    before = run_local_outputs(gates, queries, keys, values, 0)
    slices, before = lax.optimization_barrier((slices, before))
    starts = run_prefix(slices, count)
    starts, before = lax.optimization_barrier((starts, before))
    entering = swap_slices(starts, count)
    numer, stats, _ = run_local_outputs(gates, queries, keys, values, 1, before)
    parts = [None] * owners
    place = mine
    for hops, limit in zip(HOPS, FINISH_LIMITS):
        group = run_finish(place, queries, numer, gates, stats, entering, owners, hops, limit)
        for hop, hidden in zip(hops, group):
            if hop:
                hidden = lax.ppermute(hidden, "head", [(i, (i + hop) % owners) for i in range(owners)])
            parts[hop] = hidden
    return run_norm(mine, norm_gain.reshape(1, -1), parts)


def solution(mesh):
    in_specs = (
        P("seq", "head", None),
        P("seq", "head", None),
        P("seq", "head", None),
        P("head", "seq"),
        P("head", "seq"),
        P(),
    )
    out_specs = P(("seq", "head"), None)
    return jax.shard_map(shards, mesh=mesh, in_specs=in_specs, out_specs=out_specs, check_vma=False)
```

```python
import functools

import jax
import jax.numpy as jnp
from jax import lax
from jax.experimental import pallas as pl
from jax.experimental.pallas import tpu as pltpu
from jax.sharding import PartitionSpec as P

EPSILON = 1e-06
FLOOR_LOG = -1e30
L = 256
EXT = 128
BLOCKS = 4
BF = jnp.bfloat16
F32 = jnp.float32
VMEM_LIMIT = 60 * 1024 * 1024
OUTPUTS_LIMIT = 60 * 1024 * 1024
SMALL_LIMIT = 20 * 1024 * 1024
FINISH_LIMITS = (61 * 1024 * 1024, 61 * 1024 * 1024, 61 * 1024 * 1024,)
HOPS = ((4,), (3, 5), (2, 6, 1, 7, 0))


def dot(a, b):
    return jnp.dot(a, b, preferred_element_type=F32)


def pieces(x):
    hi = x.astype(BF).astype(F32)
    rest = x - hi
    mid = rest.astype(BF).astype(F32)
    return hi, mid, rest - mid


def ones_column(rows):
    return jnp.where(lax.broadcasted_iota(jnp.int32, (rows, EXT), 1) == 0, 1.0, 0.0).astype(BF)


def lay_columns(rows, columns):
    lane = lax.broadcasted_iota(jnp.int32, (rows, EXT), 1)
    out = jnp.zeros((rows, EXT), F32)
    for number, column in enumerate(columns):
        out = jnp.where(lane == number, column, out)
    return out


def gate_rows(forget_ref, input_ref, gates_ref, weight_ref, ends_ref):
    chunks = forget_ref.shape[0] * 128 // L

    def rows(ref):
        return jnp.concatenate(
            [ref[pl.ds(0, chunks, stride=2), :], ref[pl.ds(1, chunks, stride=2), :]], axis=1
        )

    forget = rows(forget_ref)
    lgate = jnp.minimum(forget, 0.0) - jnp.log1p(jnp.exp(-jnp.abs(forget)))
    lane = lax.broadcasted_iota(jnp.int32, (chunks, L), 1)
    within = lgate
    shift = 1
    while shift < L:
        within = within + jnp.where(lane >= shift, pltpu.roll(within, shift, 1), 0.0)
        shift *= 2
    lead = rows(input_ref) - within
    top = lead
    shift = 1
    while shift < L:
        top = jnp.maximum(top, jnp.where(lane >= shift, pltpu.roll(top, shift, 1), -jnp.inf))
        shift *= 2
    total = within[:, L - 1 :]
    chunk_top = total + top[:, L - 1 :]
    row = lax.broadcasted_iota(jnp.int32, (chunks, 1), 0)
    level = jnp.full((1, 1), FLOOR_LOG, F32)
    before = jnp.zeros((1, 1), F32)
    enter = jnp.zeros((chunks, 1), F32)
    leave = jnp.zeros((chunks, 1), F32)
    prefix = jnp.zeros((chunks, 1), F32)
    for c in range(chunks):
        enter = jnp.where(row == c, level, enter)
        prefix = jnp.where(row == c, before, prefix)
        level = jnp.maximum(level + total[c : c + 1], chunk_top[c : c + 1])
        before = before + total[c : c + 1]
        leave = jnp.where(row == c, level, leave)
    after = jnp.zeros((1, 1), F32)
    suffix = jnp.zeros((chunks, 1), F32)
    for c in reversed(range(chunks)):
        suffix = jnp.where(row == c, after, suffix)
        after = after + total[c : c + 1]
    carry = within + enter
    levels = jnp.maximum(within + top, carry)
    keylog = lead + total
    weight_ref[...] = jnp.exp(keylog + suffix - level)
    ends_ref[0:1, :] = jnp.broadcast_to(level, (1, 128))
    ends_ref[1:2, :] = jnp.broadcast_to(before, (1, 128))

    def put(number, value):
        for half in range(2):
            gates_ref[pl.ds(half * 8 + number, chunks, stride=16), :] = value[:, half * 128 : (half + 1) * 128]

    put(0, within - levels)
    put(1, jnp.exp(carry - levels))
    put(2, lead)
    put(3, jnp.exp(keylog - leave))
    put(4, within + prefix)
    put(5, levels)
    put(6, jnp.broadcast_to(jnp.exp(enter + total - leave), (chunks, L)))
    put(7, jnp.zeros((chunks, L), F32))


def fetch(pairs, sems):
    waits = []
    for row, blocks in enumerate(pairs):
        started = []
        for column, (source, target) in enumerate(blocks):
            copy = pltpu.make_async_copy(source, target, sems.at[row, column])
            copy.start()
            started.append(copy)
        waits.append(started)
    return waits


def local_state(
    forget_ref, input_ref, key_hbm, value_hbm, packet_ref, gates_ref, key_ref, value_ref, weight_ref, ends_ref, sems
):
    tokens, rows = key_ref.shape
    width = value_ref.shape[1]
    block = tokens // sems.shape[0]
    spans = [pl.ds(number * block, block) for number in range(sems.shape[0])]
    waits = fetch(
        [
            [(key_hbm.at[span, :], key_ref.at[span, :]), (value_hbm.at[span, :], value_ref.at[span, :])]
            for span in spans
        ],
        sems,
    )
    gate_rows(forget_ref, input_ref, gates_ref, weight_ref, ends_ref)
    ones = ones_column(block)
    per = block // L
    matrix = vector = None
    for number, span in enumerate(spans):
        for copy in waits[number]:
            copy.wait()
        weight = jnp.concatenate(
            [weight_ref[number * per + part : number * per + part + 1, :] for part in range(per)], axis=1
        )
        weighted = (key_ref[span, :].T.astype(F32) * weight).astype(BF)
        add_matrix, add_vector = dot(weighted, value_ref[span, :]), dot(weighted, ones)
        matrix = add_matrix if matrix is None else matrix + add_matrix
        vector = add_vector if vector is None else vector + add_vector
    packet_ref[:, :width] = matrix.astype(BF)
    level = pieces(ends_ref[0:1, 0:1])
    decay = pieces(ends_ref[1:2, 0:1])
    packet_ref[:, width:] = lay_columns(rows, pieces(vector[:, 0:1])[:2] + level + decay).astype(BF)


def run_local_state(forget, inputs, keys, values):
    tokens, depth = keys.shape
    width = values.shape[1]
    chunks = tokens // L
    vmem = pl.BlockSpec(memory_space=pltpu.VMEM)
    hbm = pl.BlockSpec(memory_space=pl.ANY)
    return pl.pallas_call(
        local_state,
        in_specs=[vmem, vmem, hbm, hbm],
        out_specs=[vmem, vmem],
        out_shape=[
            jax.ShapeDtypeStruct((depth, width + EXT), BF),
            jax.ShapeDtypeStruct((chunks * 16, 128), F32),
        ],
        scratch_shapes=[
            pltpu.VMEM((tokens, depth), BF),
            pltpu.VMEM((tokens, width), BF),
            pltpu.VMEM((chunks, L), F32),
            pltpu.VMEM((8, 128), F32),
            pltpu.SemaphoreType.DMA((BLOCKS, 2)),
        ],
        compiler_params=pltpu.CompilerParams(vmem_limit_bytes=VMEM_LIMIT),
        name="local_state",
    )(forget, inputs, keys, values)


def prefix_states(slices_ref, out_ref, *, count, each):
    wide = out_ref.shape[1]
    width = wide - EXT
    level = jnp.full((each, 1), FLOOR_LOG, F32)
    state = jnp.zeros((each, width), F32)
    vector = jnp.zeros((each, 1), F32)
    per = 16 // each
    for group in range(count // per):
        block = slices_ref[group * 16 : (group + 1) * 16, :].astype(F32)
        starts = []
        for number in range(per):
            mine = block[number * each : (number + 1) * each]

            def column(first, how_many):
                return sum(mine[:, width + first + n : width + first + n + 1] for n in range(how_many))

            hi, lo, _ = pieces(vector)
            starts.append(
                jnp.concatenate([state, lay_columns(each, (hi, lo) + pieces(level))], axis=1)
            )
            shifted = level + column(5, 3)
            later = column(2, 3)
            level = jnp.maximum(shifted, later)
            old, new = jnp.exp(shifted - level), jnp.exp(later - level)
            state = old * state + new * mine[:, :width]
            vector = old * vector + new * column(0, 2)
        out_ref[group * 16 : (group + 1) * 16, :] = jnp.concatenate(starts, axis=0).astype(BF)


def run_prefix(slices, count):
    rows, wide = slices.shape
    return pl.pallas_call(
        functools.partial(prefix_states, count=count, each=rows // count),
        out_shape=jax.ShapeDtypeStruct((rows, wide), BF),
        compiler_params=pltpu.CompilerParams(vmem_limit_bytes=SMALL_LIMIT),
        name="prefix_states",
    )(slices)


def local_outputs(gates_ref, query_ref, key_ref, value_ref, *refs):
    start_ref = refs[-4] if len(refs) == 6 else None
    numer_ref, stats_ref, state_ref = refs[-3:]
    width = value_ref.shape[1]

    @pl.when(pl.program_id(0) == 0)
    def _():
        state_ref[...] = jnp.zeros_like(state_ref) if start_ref is None else start_ref[...]

    per = query_ref.shape[0] // L
    scale = 1.0 / query_ref.shape[1] ** 0.5
    causal = lax.broadcasted_iota(jnp.int32, (L, L), 0) >= lax.broadcasted_iota(jnp.int32, (L, L), 1)
    ones = ones_column(L)
    for part in range(per):
        span = slice(part * L, (part + 1) * L)
        gates = jnp.concatenate(
            [gates_ref[part * 16 + half * 8 : part * 16 + half * 8 + 8, :] for half in range(2)], axis=1
        )
        columns = gates.T
        query, key, value = query_ref[span, :], key_ref[span, :], value_ref[span, :]
        key_t = key.T
        scores = dot(query, key_t) * scale
        probs = jnp.where(causal, jnp.exp(columns[:, 0:1] + gates[2:3, :]) * scores, 0.0)
        far = columns[:, 1:2] * scale
        state = state_ref[...]
        high = state.astype(BF)
        low = (state - high.astype(F32)).astype(BF)
        carried = dot(query, high) + dot(query, low)
        numer_ref[span, :] = (dot(probs.astype(BF), value) + far * carried[:, :width]).astype(BF)
        denom = jnp.sum(probs, axis=1, keepdims=True) + far * carried[:, width : width + 1]
        flat = lay_columns(L, (denom,)).T[:8]
        for half in range(2):
            first = part * 16 + half * 8
            stats_ref[first : first + 8, :] = flat[:, half * 128 : (half + 1) * 128]
        weighted = (key_t.astype(F32) * gates[3:4, :]).astype(BF)
        old = gates[6:7, 0:1]
        state_ref[:, :width] = old * state[:, :width] + dot(weighted, value)
        state_ref[:, width:] = old * state[:, width:] + dot(weighted, ones)


def run_local_outputs(gates, queries, keys, values, half, before=None):
    tokens, depth = keys.shape
    width = values.shape[1]
    block = 1024
    steps = tokens // block // 2
    first = half * steps

    def at(i):
        return (first + i, 0)

    whole = pl.BlockSpec((depth, width + EXT), lambda i: (0, 0))
    return pl.pallas_call(
        local_outputs,
        grid=(steps,),
        in_specs=[
            pl.BlockSpec((block // L * 16, 128), at),
            pl.BlockSpec((block, depth), at),
            pl.BlockSpec((block, depth), at),
            pl.BlockSpec((block, width), at),
        ]
        + ([pl.BlockSpec(memory_space=pl.ANY)] * 2 + [whole] if half else []),
        out_specs=[
            pl.BlockSpec((block, width), at),
            pl.BlockSpec((block // L * 16, 128), at),
            whole,
        ],
        out_shape=[
            jax.ShapeDtypeStruct((tokens, width), BF),
            jax.ShapeDtypeStruct((tokens // L * 16, 128), F32),
            jax.ShapeDtypeStruct((depth, width + EXT), F32),
        ],
        input_output_aliases={4: 0, 5: 1} if half else {},
        compiler_params=pltpu.CompilerParams(vmem_limit_bytes=OUTPUTS_LIMIT),
        name="local_outputs",
    )(gates, queries, keys, values, *(before or ()))


def finish(
    place_ref, query_hbm, numer_hbm, gates_hbm, stats_hbm, packet_hbm, *refs, hops, owners
):
    outs = refs[: len(hops)]
    query_ref, numer_ref, gates_ref, stats_ref, packet_ref, hidden_ref, in_sems, all_sems, out_sems = refs[len(hops) :]
    first = fetch([[(packet_hbm, packet_ref), (gates_hbm, gates_ref), (stats_hbm, stats_ref)]], all_sems)[0]
    rows = query_ref.shape[1]
    width = numer_ref.shape[2]
    scale = 1.0 / query_ref.shape[2] ** 0.5
    targets = [lax.rem(place_ref[0] + hop, owners) for hop in hops]
    blocks = []
    for number, target in enumerate(targets):
        span = pl.ds(pl.multiple_of(target * rows, rows), rows)
        blocks.append(
            [(query_hbm.at[span, :], query_ref.at[number]), (numer_hbm.at[span, :], numer_ref.at[number])]
        )
    waits = fetch(blocks, in_sems)
    for copy in first:
        copy.wait()
    ends = packet_ref[0:16, width:].astype(F32)[0:1]
    entering = ends[:, 2:3] + ends[:, 3:4] + ends[:, 4:5]
    copies = []
    for number, target in enumerate(targets):
        for copy in waits[number]:
            copy.wait()
        tall = rows // L * 16
        tile = pl.ds(pl.multiple_of(target * tall, tall), tall)
        gates, stats = gates_ref[tile, :], stats_ref[tile, :]
        row = lax.broadcasted_iota(jnp.int32, (8, L), 0)
        for part in range(rows // L):
            span = slice(part * L, (part + 1) * L)

            def rows_of(array):
                first = part * 16
                return jnp.concatenate([array[first : first + 8], array[first + 8 : first + 16]], axis=1)

            marks, sums = rows_of(gates), rows_of(stats)
            local = marks[5:6]
            carry = marks[4:5] + entering
            level = jnp.maximum(local, carry)
            own = jnp.exp(local - level)
            far = jnp.exp(carry - level) * scale
            columns = jnp.where(row == 0, own, jnp.where(row == 1, far, own * sums[0:1])).T
            own, far = columns[:, 0:1], columns[:, 1:2]
            reach = dot(query_ref[number, span, :], packet_ref[...])
            vector = reach[:, width : width + 1] + reach[:, width + 1 : width + 2]
            share = 1.0 / jnp.maximum(jnp.abs(columns[:, 2:3] + far * vector), 1.0)
            hidden_ref[number, span, :] = (
                (own * share) * numer_ref[number, span, :].astype(F32) + (far * share) * reach[:, :width]
            ).astype(BF)
        copy = pltpu.make_async_copy(hidden_ref.at[number], outs[number], out_sems.at[number])
        copy.start()
        copies.append(copy)
    for copy in copies:
        copy.wait()


def run_finish(place, queries, numer, gates, stats, packet, owners, hops, limit):
    tokens, depth = queries.shape
    width = numer.shape[1]
    rows = tokens // owners
    count = len(hops)
    anywhere = pl.BlockSpec(memory_space=pl.ANY)
    return pl.pallas_call(
        functools.partial(finish, hops=hops, owners=owners),
        in_specs=[pl.BlockSpec(memory_space=pltpu.SMEM)] + [anywhere] * 5,
        out_specs=[anywhere] * count,
        out_shape=[jax.ShapeDtypeStruct((rows, width), BF)] * count,
        scratch_shapes=[
            pltpu.VMEM((count, rows, depth), BF),
            pltpu.VMEM((count, rows, width), BF),
            pltpu.VMEM(gates.shape, F32),
            pltpu.VMEM(stats.shape, F32),
            pltpu.VMEM(packet.shape, BF),
            pltpu.VMEM((count, rows, width), BF),
            pltpu.SemaphoreType.DMA((count, 2)),
            pltpu.SemaphoreType.DMA((1, 3)),
            pltpu.SemaphoreType.DMA((count,)),
        ],
        compiler_params=pltpu.CompilerParams(vmem_limit_bytes=limit),
        cost_estimate=pl.CostEstimate(
            flops=2 * count * rows * depth * packet.shape[1],
            bytes_accessed=count * rows * (2 * depth + 4 * width),
            transcendentals=0,
        ),
        name="finish",
    )(place, queries, numer, gates, stats, packet)


def norm(place_ref, gain_ref, *refs):
    out_ref = refs[-1]
    parts = refs[:-1]
    count = len(parts)
    width = parts[0].shape[1]
    square = jnp.zeros((parts[0].shape[0], 128), F32)
    for part in parts:
        wide = part[...].astype(F32)
        wide = wide * wide
        for piece in range(width // 128):
            square = square + wide[:, piece * 128 : (piece + 1) * 128]
    mean = jnp.sum(square, axis=1, keepdims=True) / (count * width)
    factor = lax.rsqrt(mean + EPSILON)
    for hop, part in enumerate(parts):
        head = lax.rem(place_ref[0] - hop + count, count)
        columns = pl.ds(pl.multiple_of(head * width, width), width)
        out_ref[:, columns] = (part[...].astype(F32) * factor * gain_ref[:, columns]).astype(BF)


def run_norm(place, gain, parts):
    rows, width = parts[0].shape
    block = 256
    total = width * len(parts)
    return pl.pallas_call(
        norm,
        grid_spec=pltpu.PrefetchScalarGridSpec(
            num_scalar_prefetch=1,
            grid=(rows // block,),
            in_specs=[pl.BlockSpec((1, total), lambda i, place: (0, 0))]
            + [pl.BlockSpec((block, width), lambda i, place: (i, 0))] * len(parts),
            out_specs=pl.BlockSpec((block, total), lambda i, place: (i, 0)),
        ),
        out_shape=jax.ShapeDtypeStruct((rows, total), BF),
        compiler_params=pltpu.CompilerParams(vmem_limit_bytes=SMALL_LIMIT),
        name="norm",
    )(place, gain, *parts)


def swap_slices(packet, count):
    rows, wide = packet.shape
    cut = packet.reshape(count, rows // count, wide)
    return lax.all_to_all(cut, "seq", 0, 0, tiled=True).reshape(rows, wide)


def shards(queries, key_vectors, value_vectors, input_gate, forget_gate, norm_gain):
    tokens = queries.shape[0]
    queries, keys, values = (a.reshape(tokens, a.shape[2]) for a in (queries, key_vectors, value_vectors))
    forget = forget_gate.reshape(tokens // 128, 128)
    inputs = input_gate.reshape(tokens // 128, 128)
    count = lax.axis_size("seq")
    owners = lax.axis_size("head")
    mine = lax.axis_index("head").astype(jnp.int32).reshape(1)
    packet, gates = run_local_state(forget, inputs, keys, values)
    slices = swap_slices(packet, count)
    before = run_local_outputs(gates, queries, keys, values, 0)
    slices, before = lax.optimization_barrier((slices, before))
    starts = run_prefix(slices, count)
    starts, before = lax.optimization_barrier((starts, before))
    entering = swap_slices(starts, count)
    numer, stats, _ = run_local_outputs(gates, queries, keys, values, 1, before)
    parts = [None] * owners
    place = mine
    for hops, limit in zip(HOPS, FINISH_LIMITS):
        group = run_finish(place, queries, numer, gates, stats, entering, owners, hops, limit)
        for hop, hidden in zip(hops, group):
            if hop:
                hidden = lax.ppermute(hidden, "head", [(i, (i + hop) % owners) for i in range(owners)])
            parts[hop] = hidden
    return run_norm(mine, norm_gain.reshape(1, -1), parts)


def solution(mesh):
    in_specs = (
        P("seq", "head", None),
        P("seq", "head", None),
        P("seq", "head", None),
        P("head", "seq"),
        P("head", "seq"),
        P(),
    )
    out_specs = P(("seq", "head"), None)
    return jax.shard_map(shards, mesh=mesh, in_specs=in_specs, out_specs=out_specs, check_vma=False)
```
